32 devices in a mesh: prow: 4 (over z), pcol: 4 (over y, core), skc: 2 (over x).
Axes of the slice: x: 2, y: 2, z: 4, core: 2. Of those that a mesh axis runs over, the one named last changes fastest.
Arguments:
- omega: float32 [256, 3, 16, 512], P('skc', None, 'prow', 'pcol'), may hold values from -4.1 to 4.1
- elastic: float32 [16, 512], P('prow', 'pcol'), may hold values from 0.25 to 3
- prony: float32 [4, 16, 512], P(None, 'prow', 'pcol'), may hold values from 0.1 to 1
- prony_weight: float32 [4], replicated, may hold values from 0.05 to 0.5
- coupling: float32 [9, 3, 3], replicated, may hold values from -0.03 to 0.03
Outputs:
- basis: float32 [256, 3, 16, 512], P('skc', None, 'prow', 'pcol')
- factor: float32 [256, 256], replicated
- gram: float32 [256, 256], replicated
The draws below stay inside these ranges and needn't reach their ends.
All inputs are finite; a program needn't handle non-finite values.
Results may differ from the reference program's by a relative error of at most 0.001.
Values sent between devices are 32-bit elements; how exact they have to be, the bound alone decides.
A program may use at most 64 MiB of HBM per device.

```python
import math
import jax
import jax.numpy as jnp
from jax import lax

SKETCH = 256
PRONY = 4
NX = 16
NY = 512


def draw_omega(key, part):
    base_key = jax.random.fold_in(key, 11)
    noise_key = jax.random.fold_in(key, 12)
    second_key = jax.random.fold_in(key, 13)
    mix_key = jax.random.fold_in(key, 14)
    mixing = jax.random.uniform(mix_key, (SKETCH,), jnp.float32, -1.0, 1.0)
    first = 0.8 * jnp.clip(jax.random.normal(base_key, (3, NX, NY), jnp.float32), -2.5, 2.5)
    second = 0.8 * jnp.clip(jax.random.normal(second_key, (3, NX, NY), jnp.float32), -2.5, 2.5)
    noise = jnp.clip(jax.random.normal(noise_key, (SKETCH, 3, NX, NY), jnp.float32), -4.0, 4.0)
    return first[None] + mixing[:, None, None, None] * second[None] + 0.01 * noise


def draw_elastic(key, part):
    value_key = jax.random.fold_in(key, 21)
    exponent = jax.random.uniform(value_key, (NX, NY), jnp.float32, 0.0, 1.0)
    base = 0.25 * jnp.exp(exponent * math.log(4.0))
    along = jnp.arange(NX, dtype=jnp.float32) / NX
    ramp = 1.0 + along
    return base * ramp[:, None]


def steps_of(stream_key, shape, split, low, high):
    loudness, own = 1.0, jax.random.fold_in(stream_key, 6)
    for dim, shards_of in split:
        draws = jnp.exp(jax.random.uniform(jax.random.fold_in(own, dim), (shards_of,), jnp.float32, low / len(split), high / len(split)))
        loudness = loudness * jnp.repeat(draws, shape[dim] // shards_of).reshape([-1 if axis == dim else 1 for axis in range(len(shape))])
    return loudness


def setup_inputs(seed: int = 0) -> dict:
    key_of = jax.random.split(jax.random.key(seed), 6)
    return {
        "omega": draw_omega(jax.random.fold_in(key_of[5], 71), 0),
        "elastic": draw_elastic(jax.random.fold_in(key_of[5], 71), 0),
        "prony": jnp.clip(jnp.exp(math.log(1.0) - 2.3025851 * jax.random.uniform(key_of[2], (PRONY, NX, NY), jnp.float32) ** steps_of(key_of[2], (PRONY, NX, NY), ((1, 4), (2, 4)), -0.2, 0.2)), 0.1, 1.0),
        "prony_weight": jnp.clip(jnp.exp(jax.random.uniform(key_of[3], (PRONY,), jnp.float32, math.log(0.05), math.log(0.5))), 0.05, 0.5),
        "coupling": jnp.clip(jax.random.uniform(key_of[4], (9, 3, 3), jnp.float32, -0.03, 0.03), -0.03, 0.03),
    }


def stencil(field, modulus, coupling):
    extent_x = field.shape[2]
    extent_y = field.shape[3]
    padded = jnp.pad(field, ((0, 0), (0, 0), (1, 1), (1, 1)))
    summed = field
    for row_off in range(3):
        for col_off in range(3):
            window = padded[:, :, row_off:row_off + extent_x, col_off:col_off + extent_y]
            weights = coupling[3 * row_off + col_off]
            summed = summed + lax.optimization_barrier(jnp.sum(weights[None, :, :, None, None] * window[:, None, :, :, :], axis=2))
    return modulus[None, None] * summed

def reference(omega, elastic, prony, prony_weight, coupling):
    modulus = elastic + lax.optimization_barrier(jnp.sum(prony_weight[:, None, None] * prony, axis=0))
    blocks = omega.reshape(4, SKETCH // 4, 3, NX, NY)

    def twice(block_cols):
        return stencil(stencil(block_cols, modulus, coupling), modulus, coupling)
    sketched = lax.map(twice, blocks).reshape(SKETCH, 3 * NX * NY)
    gram = jnp.dot(sketched, sketched.T, precision=lax.Precision.HIGHEST) / (3 * NX * NY)
    q_mat, r_mat = jnp.linalg.qr(sketched.T)
    diag_signs = jnp.sign(jnp.diagonal(r_mat))
    root_rows = math.sqrt(3 * NX * NY)
    basis = ((q_mat * diag_signs[None, :]).T * root_rows).reshape(SKETCH, 3, NX, NY)
    factor = r_mat * diag_signs[:, None] / root_rows
    return (basis, factor, gram)
```

```python
import functools
import math

import jax
import jax.numpy as jnp
from jax import lax
from jax.experimental import pallas as pl
from jax.experimental.pallas import tpu as pltpu
from jax.sharding import PartitionSpec as P

MESH = pl.DeviceIdType.MESH
HIGHEST = lax.Precision.HIGHEST
HALF = 128


def extended(shard, sides, width):
    for axis, dim in sides:
        peers, length = (lax.axis_size(axis), shard.shape[dim])
        up = [(i, (i + 1) % peers) for i in range(peers - 1)]
        down = [(j, i) for i, j in up]
        last = lax.slice_in_dim(shard, length - width, length, axis=dim)
        leading = lax.slice_in_dim(shard, 0, width, axis=dim)
        before = lax.ppermute(last, axis, up)
        after = lax.ppermute(leading, axis, down)
        shard = jnp.concatenate([before, shard, after], axis=dim)
    return shard


def stencil(field, modulus, coupling):
    extent_x = field.shape[2]
    extent_y = field.shape[3]
    padded = extended(field, (("prow", 2), ("pcol", 3)), 1)
    summed = field
    for row_off in range(3):
        for col_off in range(3):
            window = padded[:, :, row_off : row_off + extent_x, col_off : col_off + extent_y]
            weights = coupling[3 * row_off + col_off]
            summed = summed + jnp.sum(
                weights[None, :, :, None, None] * window[:, None, :, :, :], axis=2
            )
    return modulus[None, None] * summed


def dot(a, b, dims, precision=HIGHEST):
    return lax.dot_general(
        a, b, (dims, ((), ())), precision=precision, preferred_element_type=jnp.float32
    )


NN = ((1,), (0,))
NT = ((1,), (1,))
TN = ((0,), (0,))


def reduce_kernel(planes, cols, rows, part_ref, out_ref, plane_buf, row_buf,
                  send_a, recv_a, send_b, recv_b, send_c, recv_c):
    me = lax.axis_index("pcol") * cols + lax.axis_index("skc")
    row = lax.axis_index("prow")
    chunk = part_ref.shape[0] // planes

    def at_plane(t):
        return {"pcol": t // cols, "skc": t % cols}

    def piece(ref, t):
        return ref.at[pl.ds(pl.multiple_of(t * chunk, 8), chunk)]

    others = [lax.rem(me + o, planes) for o in range(1, planes)]
    other_rows = [lax.rem(row + o, rows) for o in range(1, rows)]
    barrier = pltpu.get_barrier_semaphore()
    for t in others:
        pl.semaphore_signal(barrier, inc=1, device_id=at_plane(t), device_id_type=MESH)
    for t in other_rows:
        pl.semaphore_signal(barrier, inc=1, device_id={"prow": t}, device_id_type=MESH)
    pl.semaphore_wait(barrier, planes + rows - 2)

    def exchange(targets, where, source, target, mine, send, recv):
        sent = [
            pltpu.make_async_remote_copy(
                src_ref=source(t), dst_ref=target(mine), send_sem=send.at[t],
                recv_sem=recv.at[mine], device_id=where(t), device_id_type=MESH)
            for t in targets
        ]
        for copy in sent:
            copy.start()
        for t in targets:
            pltpu.make_async_remote_copy(
                src_ref=source(t), dst_ref=target(t), send_sem=send.at[t],
                recv_sem=recv.at[t], device_id=where(t), device_id_type=MESH).wait_recv()
        return sent

    sent = exchange(others, at_plane, lambda t: piece(part_ref, t), lambda t: plane_buf.at[t],
                    me, send_a, recv_a)
    plane_buf[me] = piece(part_ref, me)[...]
    total = plane_buf[0]
    for t in range(1, planes):
        total = total + plane_buf[t]
    row_buf[row] = total
    sent += exchange(other_rows, lambda t: {"prow": t}, lambda t: row_buf.at[row],
                     lambda t: row_buf.at[t], row, send_b, recv_b)
    total = row_buf[0]
    for t in range(1, rows):
        total = total + row_buf[t]
    piece(out_ref, me)[...] = total
    sent += exchange(others, at_plane, lambda t: piece(out_ref, me), lambda t: piece(out_ref, t),
                     me, send_c, recv_c)
    for copy in sent:
        copy.wait_send()


def reduce_all(part, name, collective_id):
    cols, rows = lax.axis_size("skc"), lax.axis_size("prow")
    planes = cols * lax.axis_size("pcol")
    chunk = part.shape[0] // planes
    dma = pltpu.SemaphoreType.DMA
    return pl.pallas_call(
        functools.partial(reduce_kernel, planes, cols, rows),
        out_shape=jax.ShapeDtypeStruct(part.shape, jnp.float32),
        in_specs=[pl.BlockSpec(memory_space=pltpu.VMEM)],
        out_specs=pl.BlockSpec(memory_space=pltpu.VMEM),
        scratch_shapes=[
            pltpu.VMEM((planes, chunk, part.shape[1]), jnp.float32),
            pltpu.VMEM((rows, chunk, part.shape[1]), jnp.float32),
            dma((planes,)), dma((planes,)), dma((rows,)), dma((rows,)),
            dma((planes,)), dma((planes,)),
        ],
        compiler_params=pltpu.CompilerParams(collective_id=collective_id, has_side_effects=True),
        name=name,
    )(part)


def eliminate(block):
    size = block.shape[0]
    tiles = size // 8
    lanes = lax.broadcasted_iota(jnp.int32, (8, size), 1)
    subs = lax.broadcasted_iota(jnp.int32, (8, size), 0)
    left = [block[8 * t : 8 * t + 8] for t in range(tiles)]
    right = [jnp.where(lanes == subs + 8 * t, 1.0, 0.0).astype(jnp.float32) for t in range(tiles)]
    for j in range(size):
        t, s = divmod(j, 8)
        row_l = jnp.broadcast_to(left[t][s : s + 1], (8, size))
        row_r = jnp.broadcast_to(right[t][s : s + 1], (8, size))
        inverse = 1.0 / jnp.broadcast_to(left[t][s : s + 1, j : j + 1], (8, size))
        for v in range(t, tiles):
            if v == t and s == 7:
                continue
            factor = jnp.broadcast_to(left[v][:, j : j + 1], (8, size)) * inverse
            if v == t:
                factor = jnp.where(subs > s, factor, 0.0)
            left[v] = left[v] - factor * row_l
            right[v] = right[v] - factor * row_r
    upper, lower = [], []
    for t in range(tiles):
        diagonal = lanes == subs + 8 * t
        pivot = jnp.sum(jnp.where(diagonal, left[t], 0.0), axis=1, keepdims=True)
        scale = lax.rsqrt(pivot)
        upper.append(jnp.where(lanes >= subs + 8 * t, left[t] * scale, 0.0))
        lower.append(right[t] * scale)
    return jnp.concatenate(upper, axis=0), jnp.concatenate(lower, axis=0)


def factorize(gram_ref):
    h = HALF
    r11, i11 = eliminate(gram_ref[0:h])
    r12 = dot(i11, gram_ref[h : 2 * h], NN)
    r22, i22 = eliminate(gram_ref[2 * h : 3 * h] - dot(r12, r12, TN))
    i21 = -dot(i22, dot(r12, i11, TN), NN)
    zero = jnp.zeros((h, h), jnp.float32)
    upper = jnp.concatenate(
        [jnp.concatenate([r11, r12], axis=1), jnp.concatenate([zero, r22], axis=1)], axis=0)
    lower = jnp.concatenate(
        [jnp.concatenate([i11, zero], axis=1), jnp.concatenate([i21, i22], axis=1)], axis=0)
    return upper, lower


def pack(block_rows):
    first, second = block_rows[:HALF], block_rows[HALF:]
    return jnp.concatenate(
        [dot(first, first, NT), dot(first, second, NT), dot(second, second, NT)], axis=0)


def first_kernel(parts, gram_ref, matrix_ref, upper_ref, ortho_ref, part_ref):
    upper, lower = factorize(gram_ref)
    upper_ref[...] = upper
    width = matrix_ref.shape[1] // parts
    mine = lax.axis_index("skc")
    for p in range(parts):
        cols = slice(p * width, (p + 1) * width)
        ortho_ref[:, cols] = dot(lower, matrix_ref[:, cols], NN)
    for p in range(parts):
        @pl.when(mine == p)
        def _():
            part_ref[...] = pack(ortho_ref[:, p * width : (p + 1) * width])


def second_kernel(scale, groups, gram_ref, upper_ref, ortho_ref, out_ref, factor_ref):
    upper, lower = factorize(gram_ref)
    factor_ref[...] = dot(upper, upper_ref[...], NN) * (1.0 / scale)
    count = lower.shape[0] // groups
    mine = lax.axis_index("skc")
    for g in range(groups):
        @pl.when(mine == g)
        def _():
            out_ref[...] = dot(lower[g * count : (g + 1) * count], ortho_ref[...], NN) * scale


def call(kernel, outs, name):
    return pl.pallas_call(
        kernel,
        out_shape=[jax.ShapeDtypeStruct(s, jnp.float32) for s in outs],
        compiler_params=pltpu.CompilerParams(vmem_limit_bytes=40 * 1024 * 1024),
        name=name,
    )


def body(omega, elastic, prony, prony_weight, coupling):
    modulus = elastic + jnp.sum(prony_weight[:, None, None] * prony, axis=0)
    sketched = stencil(stencil(omega, modulus, coupling), modulus, coupling)
    local_cols, comps, extent_x, extent_y = sketched.shape
    groups = lax.axis_size("skc")
    total_cols = local_cols * groups
    points = comps * extent_x * extent_y
    row_count = points * lax.axis_size("prow") * lax.axis_size("pcol")
    root_rows = math.sqrt(row_count)
    gathered = lax.all_gather(sketched, "skc", axis=0, tiled=True)
    matrix = gathered.reshape(total_cols, points)
    width = points // groups
    own = lax.dynamic_slice_in_dim(matrix, lax.axis_index("skc") * width, width, 1)
    gram_one = reduce_all(pack(own), "sum_first", 1)
    upper_one, ortho_once, part_two = call(
        functools.partial(first_kernel, groups),
        [(total_cols, total_cols), (total_cols, points), (3 * HALF, HALF)], "first")(
            gram_one, matrix)
    gram_two = reduce_all(part_two, "sum_second", 2)
    own_rows, factor = call(
        functools.partial(second_kernel, root_rows, groups),
        [(local_cols, points), (total_cols, total_cols)], "second")(
            gram_two, upper_one, ortho_once)
    basis = own_rows.reshape(local_cols, comps, extent_x, extent_y)
    aa, ab, bb = gram_one[:HALF], gram_one[HALF : 2 * HALF], gram_one[2 * HALF :]
    gram = jnp.concatenate(
        [jnp.concatenate([aa, ab], axis=1), jnp.concatenate([ab.T, bb], axis=1)], axis=0)
    return (basis, factor, gram / row_count)


def solution(mesh):
    in_specs = (
        P("skc", None, "prow", "pcol"),
        P("prow", "pcol"),
        P(None, "prow", "pcol"),
        P(),
        P(),
    )
    out_specs = (P("skc", None, "prow", "pcol"), P(), P())
    return jax.shard_map(body, mesh=mesh, in_specs=in_specs, out_specs=out_specs, check_vma=False)
```

```python
import functools
import math

import jax
import jax.numpy as jnp
from jax import lax
from jax.experimental import pallas as pl
from jax.experimental.pallas import tpu as pltpu
from jax.sharding import PartitionSpec as P

MESH = pl.DeviceIdType.MESH
HIGHEST = lax.Precision.HIGHEST
HALF = 128


def dot(a, b, dims, precision=HIGHEST):
    return lax.dot_general(
        a, b, (dims, ((), ())), precision=precision, preferred_element_type=jnp.float32
    )


NN = ((1,), (0,))
NT = ((1,), (1,))
TN = ((0,), (0,))


def reduce_kernel(planes, cols, rows, part_ref, out_ref, plane_buf, row_buf,
                  send_a, recv_a, send_b, recv_b, send_c, recv_c):
    me = lax.axis_index("pcol") * cols + lax.axis_index("skc")
    row = lax.axis_index("prow")
    chunk = part_ref.shape[0] // planes

    def at_plane(t):
        return {"pcol": t // cols, "skc": t % cols}

    def piece(ref, t):
        return ref.at[pl.ds(pl.multiple_of(t * chunk, 8), chunk)]

    others = [lax.rem(me + o, planes) for o in range(1, planes)]
    other_rows = [lax.rem(row + o, rows) for o in range(1, rows)]
    barrier = pltpu.get_barrier_semaphore()
    for t in others:
        pl.semaphore_signal(barrier, inc=1, device_id=at_plane(t), device_id_type=MESH)
    for t in other_rows:
        pl.semaphore_signal(barrier, inc=1, device_id={"prow": t}, device_id_type=MESH)
    pl.semaphore_wait(barrier, planes + rows - 2)

    def exchange(targets, where, source, target, mine, send, recv):
        sent = [
            pltpu.make_async_remote_copy(
                src_ref=source(t), dst_ref=target(mine), send_sem=send.at[t],
                recv_sem=recv.at[mine], device_id=where(t), device_id_type=MESH)
            for t in targets
        ]
        for copy in sent:
            copy.start()
        for t in targets:
            pltpu.make_async_remote_copy(
                src_ref=source(t), dst_ref=target(t), send_sem=send.at[t],
                recv_sem=recv.at[t], device_id=where(t), device_id_type=MESH).wait_recv()
        return sent

    sent = exchange(others, at_plane, lambda t: piece(part_ref, t), lambda t: plane_buf.at[t],
                    me, send_a, recv_a)
    plane_buf[me] = piece(part_ref, me)[...]
    total = plane_buf[0]
    for t in range(1, planes):
        total = total + plane_buf[t]
    row_buf[row] = total
    sent += exchange(other_rows, lambda t: {"prow": t}, lambda t: row_buf.at[row],
                     lambda t: row_buf.at[t], row, send_b, recv_b)
    total = row_buf[0]
    for t in range(1, rows):
        total = total + row_buf[t]
    piece(out_ref, me)[...] = total
    sent += exchange(others, at_plane, lambda t: piece(out_ref, me), lambda t: piece(out_ref, t),
                     me, send_c, recv_c)
    for copy in sent:
        copy.wait_send()


def reduce_all(part, name, collective_id):
    cols, rows = lax.axis_size("skc"), lax.axis_size("prow")
    planes = cols * lax.axis_size("pcol")
    chunk = part.shape[0] // planes
    dma = pltpu.SemaphoreType.DMA
    return pl.pallas_call(
        functools.partial(reduce_kernel, planes, cols, rows),
        out_shape=jax.ShapeDtypeStruct(part.shape, jnp.float32),
        in_specs=[pl.BlockSpec(memory_space=pltpu.VMEM)],
        out_specs=pl.BlockSpec(memory_space=pltpu.VMEM),
        scratch_shapes=[
            pltpu.VMEM((planes, chunk, part.shape[1]), jnp.float32),
            pltpu.VMEM((rows, chunk, part.shape[1]), jnp.float32),
            dma((planes,)), dma((planes,)), dma((rows,)), dma((rows,)),
            dma((planes,)), dma((planes,)),
        ],
        compiler_params=pltpu.CompilerParams(collective_id=collective_id, has_side_effects=True),
        name=name,
    )(part)


def eliminate(block):
    size = block.shape[0]
    tiles = size // 8
    lanes = lax.broadcasted_iota(jnp.int32, (8, size), 1)
    subs = lax.broadcasted_iota(jnp.int32, (8, size), 0)
    left = [block[8 * t : 8 * t + 8] for t in range(tiles)]
    right = [jnp.where(lanes == subs + 8 * t, 1.0, 0.0).astype(jnp.float32) for t in range(tiles)]

    def columns(tile, t):
        return [jnp.broadcast_to(tile[:, 8 * t + c : 8 * t + c + 1], (8, size)) for c in range(8)]

    def row(tile, s):
        return jnp.broadcast_to(tile[s : s + 1], (8, size))

    scales = []
    for t in range(tiles):
        cols = columns(left[t], t)
        inverses, pivots, rows_l, rows_r = [], [], [], []
        scale = None
        for s in range(8):
            pivot = row(cols[s], s)
            inverse = 1.0 / pivot
            scale = pivot if scale is None else jnp.where(subs == s, pivot, scale)
            rows_l.append(row(left[t], s))
            rows_r.append(row(right[t], s))
            inverses.append(inverse)
            if s == 7:
                pivots.append([])
                break
            factor = jnp.where(subs > s, cols[s] * inverse, 0.0)
            heads = [row(cols[c], s) for c in range(s + 1, 8)]
            pivots.append(heads)
            for c in range(s + 1, 8):
                cols[c] = cols[c] - factor * heads[c - s - 1]
            left[t] = left[t] - factor * rows_l[s]
            right[t] = right[t] - factor * rows_r[s]
        scales.append(lax.rsqrt(scale))
        for v in range(t + 1, tiles):
            cols = columns(left[v], t)
            for s in range(8):
                factor = cols[s] * inverses[s]
                for c in range(s + 1, 8):
                    cols[c] = cols[c] - factor * pivots[s][c - s - 1]
                left[v] = left[v] - factor * rows_l[s]
                right[v] = right[v] - factor * rows_r[s]
    upper = [jnp.where(lanes >= subs + 8 * t, left[t] * scales[t], 0.0) for t in range(tiles)]
    lower = [right[t] * scales[t] for t in range(tiles)]
    return jnp.concatenate(upper, axis=0), jnp.concatenate(lower, axis=0)


def factorize(gram_ref):
    h = HALF
    r11, i11 = eliminate(gram_ref[0:h])
    r12 = dot(i11, gram_ref[h : 2 * h], NN)
    r22, i22 = eliminate(gram_ref[2 * h : 3 * h] - dot(r12, r12, TN))
    i21 = -dot(i22, dot(r12, i11, TN), NN)
    zero = jnp.zeros((h, h), jnp.float32)
    upper = jnp.concatenate(
        [jnp.concatenate([r11, r12], axis=1), jnp.concatenate([zero, r22], axis=1)], axis=0)
    lower = jnp.concatenate(
        [jnp.concatenate([i11, zero], axis=1), jnp.concatenate([i21, i22], axis=1)], axis=0)
    return upper, lower


def sketch_kernel(cols, rows, planes, field_ref, modulus_ref, coupling_ref,
                  matrix_ref, part_ref, once, above, below, edges, arrived, halo,
                  send_row, recv_row, send_col, recv_col, send_skc, recv_skc):
    extent, comps, count, width = field_ref.shape
    blocks = extent * comps
    mine = lax.axis_index("skc")
    row, col = lax.axis_index("prow"), lax.axis_index("pcol")
    has = {-1: row > 0, 0: None, 1: row < rows - 1}
    has_col = {-1: col > 0, 1: col < planes - 1}
    corners = [(a, b) for b in (-1, 1) for a in (-1, 0, 1)]

    def exists(a, b):
        if b == 0:
            return has[a]
        return has_col[b] if a == 0 else jnp.logical_and(has[a], has_col[b])

    def at(a, b):
        return {"prow": row + a, "pcol": col + b}

    def skc_peer(o):
        return lax.rem(mine + o, cols)

    directions = corners + [(-1, 0), (1, 0)]
    above[...] = jnp.zeros_like(above)
    below[...] = jnp.zeros_like(below)
    arrived[...] = jnp.zeros_like(arrived)
    barrier = pltpu.get_barrier_semaphore()
    for a, b in directions:
        @pl.when(exists(a, b))
        def _():
            pl.semaphore_signal(barrier, inc=1, device_id=at(a, b), device_id_type=MESH)
    for o in range(1, cols):
        pl.semaphore_signal(barrier, inc=1, device_id={"skc": skc_peer(o)}, device_id_type=MESH)
    ends = [jnp.where(row > 0, 1, 0) + jnp.where(row < rows - 1, 1, 0),
            jnp.where(col > 0, 1, 0) + jnp.where(col < planes - 1, 1, 0)]
    pl.semaphore_wait(barrier, (ends[0] + 1) * (ends[1] + 1) - 1 + cols - 1)

    lanes = lax.broadcasted_iota(jnp.int32, (8, width), 1)
    wide = lax.broadcasted_iota(jnp.int32, (count, width), 1)

    def row_copy(source, step, a):
        index = 2 * step + (0 if a < 0 else 1)
        target = below if a < 0 else above
        return pltpu.make_async_remote_copy(
            src_ref=source.at[0 if a < 0 else extent - 1], dst_ref=target.at[step],
            send_sem=send_row.at[index], recv_sem=recv_row.at[index],
            device_id=at(a, 0), device_id_type=MESH)

    def col_copy(step, a, b):
        index = 6 * step + corners.index((a, b))
        return pltpu.make_async_remote_copy(
            src_ref=edges.at[2 * step + (0 if b < 0 else 1)], dst_ref=arrived.at[index],
            send_sem=send_col.at[index], recv_sem=recv_col.at[index],
            device_id=at(a, b), device_id_type=MESH)

    def exchange(source, step):
        for a in (-1, 1):
            @pl.when(exists(a, 0))
            def _():
                row_copy(source, step, a).start()
        for b in (-1, 1):
            packed = jnp.zeros((count, width), jnp.float32)
            for p in range(blocks):
                place = source[p // comps, p % comps]
                edge = place[:, 0:1] if b < 0 else place[:, width - 1 : width]
                packed = jnp.where(wide == p, edge, packed)
            edges[2 * step + (0 if b < 0 else 1)] = packed.T[: edges.shape[1]]
        for a, b in corners:
            @pl.when(exists(a, b))
            def _():
                col_copy(step, a, b).start()
        for a, b in corners:
            @pl.when(exists(-a, -b))
            def _():
                col_copy(step, a, b).wait_recv()
        pad = jnp.zeros((width - blocks - 2 * comps, count), jnp.float32)
        for b in (-1, 1):
            index = 6 * step
            centre = arrived[index + corners.index((0, b))][:blocks]
            upper = arrived[index + corners.index((1, b))][blocks - comps : blocks]
            under = arrived[index + corners.index((-1, b))][:comps]
            halo[0 if b > 0 else 1] = jnp.concatenate([upper, centre, under, pad], axis=0).T
        for a in (-1, 1):
            @pl.when(exists(-a, 0))
            def _():
                row_copy(source, step, a).wait_recv()

    def apply(source, step, store):
        def tile(k, carry):
            at_k = pl.ds(pl.multiple_of(k * 8, 8), 8)
            acc = [[source[x, i, at_k] for x in range(extent)] for i in range(comps)]
            before, after = halo[0, at_k], halo[1, at_k]
            for j in range(comps):
                plain = [above[step, j, at_k]] + [source[x, j, at_k] for x in range(extent)]
                plain.append(below[step, j, at_k])
                for c in range(3):
                    if c == 1:
                        shifted = plain
                    else:
                        edge, hide, turn = (before, 0, 1) if c == 0 else (after, width - 1, width - 1)
                        shifted = [
                            jnp.where(lanes == hide, edge[:, comps * x + j : comps * x + j + 1],
                                      pltpu.roll(plain[x], turn, 1))
                            for x in range(extent + 2)
                        ]
                    for r in range(3):
                        for i in range(comps):
                            weight = coupling_ref[(3 * r + c) * comps * comps + i * comps + j]
                            for x in range(extent):
                                acc[i][x] = acc[i][x] + weight * shifted[x + r]
            for i in range(comps):
                for x in range(extent):
                    store(x, i, k, modulus_ref[x : x + 1, :] * acc[i][x])
            return carry

        lax.fori_loop(0, count // 8, tile, 0)

    def store_once(x, i, k, value):
        once[x, i, pl.ds(pl.multiple_of(k * 8, 8), 8)] = value

    def store_last(x, i, k, value):
        start = pl.multiple_of(mine * count + k * 8, 8)
        matrix_ref[comps * x + i, pl.ds(start, 8)] = value

    exchange(field_ref, 0)
    apply(field_ref, 0, store_once)
    exchange(once, 1)
    apply(once, 1, store_last)

    share = blocks // cols

    def skc_copy(owner, to, part, o):
        place = matrix_ref.at[pl.ds(part * share, share), pl.ds(pl.multiple_of(owner * count, 8), count)]
        return pltpu.make_async_remote_copy(
            src_ref=place, dst_ref=place, send_sem=send_skc.at[o], recv_sem=recv_skc.at[o],
            device_id={"skc": to}, device_id_type=MESH)

    pairs = [(q, o) for q in range(cols) for o in range(1, cols)]
    for n, (q, o) in enumerate(pairs):
        to = skc_peer(o)
        skc_copy(mine, to, lax.rem(to + q, cols), n).start()
    for n, (q, o) in enumerate(pairs[: cols - 1]):
        owner = lax.rem(mine + cols - o, cols)
        skc_copy(owner, owner, mine, n).wait_recv()
    part_ref[...] = pack_blocks(matrix_ref, mine * share, share)
    for n, (q, o) in enumerate(pairs):
        if q > 0:
            owner = lax.rem(mine + cols - o, cols)
            skc_copy(owner, owner, lax.rem(mine + q, cols), n).wait_recv()
    for n, (q, o) in enumerate(pairs):
        to = skc_peer(o)
        skc_copy(mine, to, lax.rem(to + q, cols), n).wait_send()
    for step in range(2):
        source = field_ref if step == 0 else once
        for a in (-1, 1):
            @pl.when(exists(a, 0))
            def _():
                row_copy(source, step, a).wait_send()
        for a, b in corners:
            @pl.when(exists(a, b))
            def _():
                col_copy(step, a, b).wait_send()


def pack_blocks(ref, start, share):
    total = None
    for p in range(share):
        block = ref[start + p]
        first, second = block[:HALF], block[HALF:]
        terms = [dot(first, first, NT), dot(first, second, NT), dot(second, second, NT)]
        total = terms if total is None else [s + t for s, t in zip(total, terms)]
    return jnp.concatenate(total, axis=0)


def sketch(field, modulus, coupling):
    extent, comps, count, width = field.shape
    cols, rows, planes = (lax.axis_size(a) for a in ("skc", "prow", "pcol"))
    blocks = extent * comps
    edge_rows = -(-blocks // 8) * 8
    dma = pltpu.SemaphoreType.DMA
    vmem = pl.BlockSpec(memory_space=pltpu.VMEM)
    f32 = jnp.float32
    return pl.pallas_call(
        functools.partial(sketch_kernel, cols, rows, planes),
        out_shape=[
            jax.ShapeDtypeStruct((blocks, count * cols, width), f32),
            jax.ShapeDtypeStruct((3 * HALF, HALF), f32),
        ],
        in_specs=[vmem, vmem, pl.BlockSpec(memory_space=pltpu.SMEM)],
        out_specs=[vmem, vmem],
        scratch_shapes=[
            pltpu.VMEM((extent, comps, count, width), f32),
            pltpu.VMEM((2, comps, count, width), f32),
            pltpu.VMEM((2, comps, count, width), f32),
            pltpu.VMEM((4, edge_rows, count), f32),
            pltpu.VMEM((12, edge_rows, count), f32),
            pltpu.VMEM((2, count, width), f32),
            dma((4,)), dma((4,)), dma((12,)), dma((12,)),
            dma((cols * (cols - 1),)), dma((cols * (cols - 1),)),
        ],
        compiler_params=pltpu.CompilerParams(
            collective_id=3, has_side_effects=True, vmem_limit_bytes=40 * 1024 * 1024),
        name="sketch",
    )(field, modulus, coupling)


def first_kernel(groups, gram_ref, matrix_ref, upper_ref, ortho_ref, part_ref):
    upper, lower = factorize(gram_ref)
    upper_ref[...] = upper
    blocks = matrix_ref.shape[0]
    for p in range(blocks):
        ortho_ref[p] = dot(lower, matrix_ref[p], NN)
    share = blocks // groups
    part_ref[...] = pack_blocks(ortho_ref, lax.axis_index("skc") * share, share)


def second_kernel(scale, groups, gram_ref, upper_ref, ortho_ref, out_ref, factor_ref, lower_ref):
    upper, lower = factorize(gram_ref)
    factor_ref[...] = dot(upper, upper_ref[...], NN) * (1.0 / scale)
    count = lower.shape[0] // groups
    lower_ref[...] = lower * scale
    own = lower_ref[pl.ds(pl.multiple_of(lax.axis_index("skc") * count, 8), count)]
    for p in range(ortho_ref.shape[0]):
        out_ref[p] = dot(own, ortho_ref[p], NN)


def call(kernel, outs, name, scratch=()):
    return pl.pallas_call(
        kernel,
        out_shape=[jax.ShapeDtypeStruct(s, jnp.float32) for s in outs],
        scratch_shapes=[pltpu.VMEM(s, jnp.float32) for s in scratch],
        compiler_params=pltpu.CompilerParams(vmem_limit_bytes=40 * 1024 * 1024),
        name=name,
    )


def body(omega, elastic, prony, prony_weight, coupling):
    modulus = elastic + jnp.sum(prony_weight[:, None, None] * prony, axis=0)
    local_cols, comps, extent_x, extent_y = omega.shape
    groups = lax.axis_size("skc")
    total_cols = local_cols * groups
    blocks = comps * extent_x
    row_count = blocks * extent_y * lax.axis_size("prow") * lax.axis_size("pcol")
    root_rows = math.sqrt(row_count)
    matrix, part_one = sketch(omega.transpose(2, 1, 0, 3), modulus, coupling.reshape(-1))
    gram_one = reduce_all(part_one, "sum_first", 1)
    square = (total_cols, total_cols)
    upper_one, ortho_once, part_two = call(
        functools.partial(first_kernel, groups),
        [square, matrix.shape, (3 * HALF, HALF)], "first")(gram_one, matrix)
    gram_two = reduce_all(part_two, "sum_second", 2)
    own_rows, factor = call(
        functools.partial(second_kernel, root_rows, groups),
        [(blocks, local_cols, extent_y), square], "second", [square])(
            gram_two, upper_one, ortho_once)
    basis = own_rows.reshape(extent_x, comps, local_cols, extent_y).transpose(2, 1, 0, 3)
    aa, ab, bb = gram_one[:HALF], gram_one[HALF : 2 * HALF], gram_one[2 * HALF :]
    gram = jnp.concatenate(
        [jnp.concatenate([aa, ab], axis=1), jnp.concatenate([ab.T, bb], axis=1)], axis=0)
    return (basis, factor, gram / row_count)


def solution(mesh):
    in_specs = (
        P("skc", None, "prow", "pcol"),
        P("prow", "pcol"),
        P(None, "prow", "pcol"),
        P(),
        P(),
    )
    out_specs = (P("skc", None, "prow", "pcol"), P(), P())
    return jax.shard_map(body, mesh=mesh, in_specs=in_specs, out_specs=out_specs, check_vma=False)
```

```python
import functools
import math

import jax
import jax.numpy as jnp
from jax import lax
from jax.experimental import pallas as pl
from jax.experimental.pallas import tpu as pltpu
from jax.sharding import PartitionSpec as P

MESH = pl.DeviceIdType.MESH
HIGHEST = lax.Precision.HIGHEST
HALF = 128


def dot(a, b, dims, precision=HIGHEST):
    return lax.dot_general(
        a, b, (dims, ((), ())), precision=precision, preferred_element_type=jnp.float32
    )


NN = ((1,), (0,))
NT = ((1,), (1,))
TN = ((0,), (0,))


def reduce_kernel(planes, cols, rows, part_ref, out_ref, plane_buf, row_buf,
                  send_a, recv_a, send_b, recv_b, send_c, recv_c):
    me = lax.axis_index("pcol") * cols + lax.axis_index("skc")
    row = lax.axis_index("prow")
    chunk = part_ref.shape[0] // planes

    def at_plane(t):
        return {"pcol": t // cols, "skc": t % cols}

    def piece(ref, t):
        return ref.at[pl.ds(pl.multiple_of(t * chunk, 8), chunk)]

    others = [lax.rem(me + o, planes) for o in range(1, planes)]
    other_rows = [lax.rem(row + o, rows) for o in range(1, rows)]
    barrier = pltpu.get_barrier_semaphore()
    for t in others:
        pl.semaphore_signal(barrier, inc=1, device_id=at_plane(t), device_id_type=MESH)
    for t in other_rows:
        pl.semaphore_signal(barrier, inc=1, device_id={"prow": t}, device_id_type=MESH)
    pl.semaphore_wait(barrier, planes + rows - 2)

    def exchange(targets, where, source, target, mine, send, recv):
        sent = [
            pltpu.make_async_remote_copy(
                src_ref=source(t), dst_ref=target(mine), send_sem=send.at[t],
                recv_sem=recv.at[mine], device_id=where(t), device_id_type=MESH)
            for t in targets
        ]
        for copy in sent:
            copy.start()
        for t in targets:
            pltpu.make_async_remote_copy(
                src_ref=source(t), dst_ref=target(t), send_sem=send.at[t],
                recv_sem=recv.at[t], device_id=where(t), device_id_type=MESH).wait_recv()
        return sent

    sent = exchange(others, at_plane, lambda t: piece(part_ref, t), lambda t: plane_buf.at[t],
                    me, send_a, recv_a)
    plane_buf[me] = piece(part_ref, me)[...]
    total = plane_buf[0]
    for t in range(1, planes):
        total = total + plane_buf[t]
    row_buf[row] = total
    sent += exchange(other_rows, lambda t: {"prow": t}, lambda t: row_buf.at[row],
                     lambda t: row_buf.at[t], row, send_b, recv_b)
    total = row_buf[0]
    for t in range(1, rows):
        total = total + row_buf[t]
    piece(out_ref, me)[...] = total
    sent += exchange(others, at_plane, lambda t: piece(out_ref, me), lambda t: piece(out_ref, t),
                     me, send_c, recv_c)
    for copy in sent:
        copy.wait_send()


def reduce_all(part, name, collective_id):
    cols, rows = lax.axis_size("skc"), lax.axis_size("prow")
    planes = cols * lax.axis_size("pcol")
    chunk = part.shape[0] // planes
    dma = pltpu.SemaphoreType.DMA
    return pl.pallas_call(
        functools.partial(reduce_kernel, planes, cols, rows),
        out_shape=jax.ShapeDtypeStruct(part.shape, jnp.float32),
        in_specs=[pl.BlockSpec(memory_space=pltpu.VMEM)],
        out_specs=pl.BlockSpec(memory_space=pltpu.VMEM),
        scratch_shapes=[
            pltpu.VMEM((planes, chunk, part.shape[1]), jnp.float32),
            pltpu.VMEM((rows, chunk, part.shape[1]), jnp.float32),
            dma((planes,)), dma((planes,)), dma((rows,)), dma((rows,)),
            dma((planes,)), dma((planes,)),
        ],
        compiler_params=pltpu.CompilerParams(collective_id=collective_id, has_side_effects=True),
        name=name,
    )(part)


def eliminate(block):
    size = block.shape[0]
    tiles = size // 8
    lanes = lax.broadcasted_iota(jnp.int32, (8, size), 1)
    subs = lax.broadcasted_iota(jnp.int32, (8, size), 0)
    left = [block[8 * t : 8 * t + 8] for t in range(tiles)]
    right = [jnp.where(lanes == subs + 8 * t, 1.0, 0.0).astype(jnp.float32) for t in range(tiles)]

    def columns(tile, t):
        return [jnp.broadcast_to(tile[:, 8 * t + c : 8 * t + c + 1], (8, size)) for c in range(8)]

    def row(tile, s):
        return jnp.broadcast_to(tile[s : s + 1], (8, size))

    scales = []
    for t in range(tiles):
        cols = columns(left[t], t)
        inverses, pivots, rows_l, rows_r = [], [], [], []
        scale = None
        for s in range(8):
            pivot = row(cols[s], s)
            inverse = 1.0 / pivot
            scale = pivot if scale is None else jnp.where(subs == s, pivot, scale)
            rows_l.append(row(left[t], s))
            rows_r.append(row(right[t], s))
            inverses.append(inverse)
            if s == 7:
                pivots.append([])
                break
            factor = jnp.where(subs > s, cols[s] * inverse, 0.0)
            heads = [row(cols[c], s) for c in range(s + 1, 8)]
            pivots.append(heads)
            for c in range(s + 1, 8):
                cols[c] = cols[c] - factor * heads[c - s - 1]
            left[t] = left[t] - factor * rows_l[s]
            right[t] = right[t] - factor * rows_r[s]
        scales.append(lax.rsqrt(scale))
        for v in range(t + 1, tiles):
            cols = columns(left[v], t)
            for s in range(8):
                factor = cols[s] * inverses[s]
                for c in range(s + 1, 8):
                    cols[c] = cols[c] - factor * pivots[s][c - s - 1]
                left[v] = left[v] - factor * rows_l[s]
                right[v] = right[v] - factor * rows_r[s]
    upper = [jnp.where(lanes >= subs + 8 * t, left[t] * scales[t], 0.0) for t in range(tiles)]
    lower = [right[t] * scales[t] for t in range(tiles)]
    return jnp.concatenate(upper, axis=0), jnp.concatenate(lower, axis=0)


def factorize(gram_ref):
    h = HALF
    r11, i11 = eliminate(gram_ref[0:h])
    r12 = dot(i11, gram_ref[h : 2 * h], NN)
    r22, i22 = eliminate(gram_ref[2 * h : 3 * h] - dot(r12, r12, TN))
    i21 = -dot(i22, dot(r12, i11, TN), NN)
    zero = jnp.zeros((h, h), jnp.float32)
    upper = jnp.concatenate(
        [jnp.concatenate([r11, r12], axis=1), jnp.concatenate([zero, r22], axis=1)], axis=0)
    lower = jnp.concatenate(
        [jnp.concatenate([i11, zero], axis=1), jnp.concatenate([i21, i22], axis=1)], axis=0)
    return upper, lower


def sketch_kernel(cols, rows, planes, field_ref, modulus_ref, coupling_ref,
                  matrix_ref, part_ref, once, above, below, edges, arrived, halo,
                  send_row, recv_row, send_col, recv_col, send_skc, recv_skc):
    extent, comps, count, width = field_ref.shape
    blocks = extent * comps
    mine = lax.axis_index("skc")
    row, col = lax.axis_index("prow"), lax.axis_index("pcol")
    has = {-1: row > 0, 0: None, 1: row < rows - 1}
    has_col = {-1: col > 0, 1: col < planes - 1}
    corners = [(a, b) for b in (-1, 1) for a in (-1, 0, 1)]

    def exists(a, b):
        if b == 0:
            return has[a]
        return has_col[b] if a == 0 else jnp.logical_and(has[a], has_col[b])

    def at(a, b):
        return {"prow": row + a, "pcol": col + b}

    def skc_peer(o):
        return lax.rem(mine + o, cols)

    directions = corners + [(-1, 0), (1, 0)]
    above[...] = jnp.zeros_like(above)
    below[...] = jnp.zeros_like(below)
    arrived[...] = jnp.zeros_like(arrived)
    barrier = pltpu.get_barrier_semaphore()
    for a, b in directions:
        @pl.when(exists(a, b))
        def _():
            pl.semaphore_signal(barrier, inc=1, device_id=at(a, b), device_id_type=MESH)
    for o in range(1, cols):
        pl.semaphore_signal(barrier, inc=1, device_id={"skc": skc_peer(o)}, device_id_type=MESH)
    ends = [jnp.where(row > 0, 1, 0) + jnp.where(row < rows - 1, 1, 0),
            jnp.where(col > 0, 1, 0) + jnp.where(col < planes - 1, 1, 0)]
    pl.semaphore_wait(barrier, (ends[0] + 1) * (ends[1] + 1) - 1 + cols - 1)

    lanes = lax.broadcasted_iota(jnp.int32, (8, width), 1)
    wide = lax.broadcasted_iota(jnp.int32, (count, width), 1)

    def row_copy(source, step, a):
        index = 2 * step + (0 if a < 0 else 1)
        target = below if a < 0 else above
        return pltpu.make_async_remote_copy(
            src_ref=source.at[0 if a < 0 else extent - 1], dst_ref=target.at[step],
            send_sem=send_row.at[index], recv_sem=recv_row.at[index],
            device_id=at(a, 0), device_id_type=MESH)

    def col_copy(step, a, b):
        index = 6 * step + corners.index((a, b))
        return pltpu.make_async_remote_copy(
            src_ref=edges.at[2 * step + (0 if b < 0 else 1)], dst_ref=arrived.at[index],
            send_sem=send_col.at[index], recv_sem=recv_col.at[index],
            device_id=at(a, b), device_id_type=MESH)

    def exchange(source, step):
        for a in (-1, 1):
            @pl.when(exists(a, 0))
            def _():
                row_copy(source, step, a).start()
        for b in (-1, 1):
            packed = jnp.zeros((count, width), jnp.float32)
            for p in range(blocks):
                place = source[p // comps, p % comps]
                edge = place[:, 0:1] if b < 0 else place[:, width - 1 : width]
                packed = jnp.where(wide == p, edge, packed)
            edges[2 * step + (0 if b < 0 else 1)] = packed.T[: edges.shape[1]]
        for a, b in corners:
            @pl.when(exists(a, b))
            def _():
                col_copy(step, a, b).start()
        for a, b in corners:
            @pl.when(exists(-a, -b))
            def _():
                col_copy(step, a, b).wait_recv()
        pad = jnp.zeros((width - blocks - 2 * comps, count), jnp.float32)
        for b in (-1, 1):
            index = 6 * step
            centre = arrived[index + corners.index((0, b))][:blocks]
            upper = arrived[index + corners.index((1, b))][blocks - comps : blocks]
            under = arrived[index + corners.index((-1, b))][:comps]
            halo[0 if b > 0 else 1] = jnp.concatenate([upper, centre, under, pad], axis=0).T
        for a in (-1, 1):
            @pl.when(exists(-a, 0))
            def _():
                row_copy(source, step, a).wait_recv()

    def apply(source, step, store):
        def tile(k, carry):
            at_k = pl.ds(pl.multiple_of(k * 8, 8), 8)
            acc = [[source[x, i, at_k] for x in range(extent)] for i in range(comps)]
            before, after = halo[0, at_k], halo[1, at_k]
            for j in range(comps):
                plain = [above[step, j, at_k]] + [source[x, j, at_k] for x in range(extent)]
                plain.append(below[step, j, at_k])
                for c in range(3):
                    if c == 1:
                        shifted = plain
                    else:
                        edge, hide, turn = (before, 0, 1) if c == 0 else (after, width - 1, width - 1)
                        shifted = [
                            jnp.where(lanes == hide, edge[:, comps * x + j : comps * x + j + 1],
                                      pltpu.roll(plain[x], turn, 1))
                            for x in range(extent + 2)
                        ]
                    for r in range(3):
                        for i in range(comps):
                            weight = coupling_ref[(3 * r + c) * comps * comps + i * comps + j]
                            for x in range(extent):
                                acc[i][x] = acc[i][x] + weight * shifted[x + r]
            for i in range(comps):
                for x in range(extent):
                    store(x, i, k, modulus_ref[x : x + 1, :] * acc[i][x])
            return carry

        lax.fori_loop(0, count // 8, tile, 0)

    def store_once(x, i, k, value):
        once[x, i, pl.ds(pl.multiple_of(k * 8, 8), 8)] = value

    def store_last(x, i, k, value):
        start = pl.multiple_of(mine * count + k * 8, 8)
        matrix_ref[comps * x + i, pl.ds(start, 8)] = value

    exchange(field_ref, 0)
    apply(field_ref, 0, store_once)
    exchange(once, 1)
    apply(once, 1, store_last)

    share = blocks // cols

    def skc_copy(owner, to, part, o):
        place = matrix_ref.at[pl.ds(part * share, share), pl.ds(pl.multiple_of(owner * count, 8), count)]
        return pltpu.make_async_remote_copy(
            src_ref=place, dst_ref=place, send_sem=send_skc.at[o], recv_sem=recv_skc.at[o],
            device_id={"skc": to}, device_id_type=MESH)

    pairs = [(0, o) for o in range(1, cols)]
    for n, (q, o) in enumerate(pairs):
        to = skc_peer(o)
        skc_copy(mine, to, lax.rem(to + q, cols), n).start()
    for n, (q, o) in enumerate(pairs[: cols - 1]):
        owner = lax.rem(mine + cols - o, cols)
        skc_copy(owner, owner, mine, n).wait_recv()
    part_ref[...] = pack_blocks(matrix_ref, mine * share, share)
    for n, (q, o) in enumerate(pairs):
        to = skc_peer(o)
        skc_copy(mine, to, lax.rem(to + q, cols), n).wait_send()
    for step in range(2):
        source = field_ref if step == 0 else once
        for a in (-1, 1):
            @pl.when(exists(a, 0))
            def _():
                row_copy(source, step, a).wait_send()
        for a, b in corners:
            @pl.when(exists(a, b))
            def _():
                col_copy(step, a, b).wait_send()


def pack_blocks(ref, start, share):
    total = None
    for p in range(share):
        block = ref[start + p]
        first, second = block[:HALF], block[HALF:]
        terms = [dot(first, first, NT), dot(first, second, NT), dot(second, second, NT)]
        total = terms if total is None else [s + t for s, t in zip(total, terms)]
    return jnp.concatenate(total, axis=0)


def sketch(field, modulus, coupling):
    extent, comps, count, width = field.shape
    cols, rows, planes = (lax.axis_size(a) for a in ("skc", "prow", "pcol"))
    blocks = extent * comps
    edge_rows = -(-blocks // 8) * 8
    dma = pltpu.SemaphoreType.DMA
    vmem = pl.BlockSpec(memory_space=pltpu.VMEM)
    f32 = jnp.float32
    return pl.pallas_call(
        functools.partial(sketch_kernel, cols, rows, planes),
        out_shape=[
            jax.ShapeDtypeStruct((blocks, count * cols, width), f32),
            jax.ShapeDtypeStruct((3 * HALF, HALF), f32),
        ],
        in_specs=[vmem, vmem, pl.BlockSpec(memory_space=pltpu.SMEM)],
        out_specs=[vmem, vmem],
        scratch_shapes=[
            pltpu.VMEM((extent, comps, count, width), f32),
            pltpu.VMEM((2, comps, count, width), f32),
            pltpu.VMEM((2, comps, count, width), f32),
            pltpu.VMEM((4, edge_rows, count), f32),
            pltpu.VMEM((12, edge_rows, count), f32),
            pltpu.VMEM((2, count, width), f32),
            dma((4,)), dma((4,)), dma((12,)), dma((12,)),
            dma((cols - 1,)), dma((cols - 1,)),
        ],
        compiler_params=pltpu.CompilerParams(
            collective_id=3, has_side_effects=True, vmem_limit_bytes=40 * 1024 * 1024),
        name="sketch",
    )(field, modulus, coupling)


def first_kernel(groups, gram_ref, matrix_ref, upper_ref, lower_ref, ortho_ref, part_ref):
    upper, lower = factorize(gram_ref)
    upper_ref[...] = upper
    lower_ref[...] = lower
    share = matrix_ref.shape[0] // groups
    start = lax.axis_index("skc") * share
    for p in range(share):
        ortho_ref[p] = dot(lower, matrix_ref[start + p], NN)
    part_ref[...] = pack_blocks(ortho_ref, 0, share)


def second_kernel(scale, groups, gram_ref, upper_one_ref, lower_one_ref, ortho_ref, matrix_ref,
                  *refs):
    rest, (out_ref, factor_ref, lower_ref, block_ref) = refs[: groups - 1], refs[groups - 1 :]
    upper, lower = factorize(gram_ref)
    factor_ref[...] = dot(upper, upper_one_ref[...], NN) * (1.0 / scale)
    count = lower.shape[0] // groups
    mine = lax.axis_index("skc")
    share = ortho_ref.shape[0]
    lower_ref[...] = lower * scale
    place = pl.ds(pl.multiple_of(mine * count, 8), count)
    own = lower_ref[place]
    for p in range(share):
        out_ref[mine * share + p] = dot(own, ortho_ref[p], NN)
    both = dot(own, lower_one_ref[...], NN)
    for q in range(1, groups):
        start = lax.rem(mine + q, groups) * share
        for p in range(share):
            slot = (q - 1) * share + p
            block_ref[slot, place] = matrix_ref[start + p, place]
            for o in range(1, groups):
                owner = lax.rem(mine + groups - o, groups)
                there = pl.ds(pl.multiple_of(owner * count, 8), count)
                block_ref[slot, there] = rest[o - 1][slot]
            out_ref[start + p] = dot(both, block_ref[slot], NN)


def call(kernel, outs, name, scratch=()):
    return pl.pallas_call(
        kernel,
        out_shape=[jax.ShapeDtypeStruct(s, jnp.float32) for s in outs],
        scratch_shapes=[pltpu.VMEM(s, jnp.float32) for s in scratch],
        compiler_params=pltpu.CompilerParams(vmem_limit_bytes=40 * 1024 * 1024),
        cost_estimate=pl.CostEstimate(
            flops=5 * 10**9, bytes_accessed=4 * 10**7, transcendentals=0),
        name=name,
    )


def remaining(matrix, count, groups):
    share = matrix.shape[0] // groups
    mine = lax.axis_index("skc")
    for offset in range(1, groups):
        to = lax.rem(mine + offset, groups)
        pieces = [
            lax.dynamic_slice(
                matrix, (lax.rem(to + q, groups) * share, mine * count, 0),
                (share, count, matrix.shape[2]))
            for q in range(1, groups)
        ]
        payload = pieces[0] if groups == 2 else jnp.concatenate(pieces, axis=0)
        yield lax.ppermute(payload, "skc", [(i, (i + offset) % groups) for i in range(groups)])


def body(omega, elastic, prony, prony_weight, coupling):
    modulus = elastic + jnp.sum(prony_weight[:, None, None] * prony, axis=0)
    local_cols, comps, extent_x, extent_y = omega.shape
    groups = lax.axis_size("skc")
    total_cols = local_cols * groups
    blocks = comps * extent_x
    row_count = blocks * extent_y * lax.axis_size("prow") * lax.axis_size("pcol")
    root_rows = math.sqrt(row_count)
    matrix, part_one = sketch(omega.transpose(2, 1, 0, 3), modulus, coupling.reshape(-1))
    gram_one = reduce_all(part_one, "sum_first", 1)
    gram_one, later = lax.optimization_barrier((gram_one, matrix))
    rest = list(remaining(later, local_cols, groups))
    square = (total_cols, total_cols)
    share = blocks // groups
    upper_one, lower_one, ortho_once, part_two = call(
        functools.partial(first_kernel, groups),
        [square, square, (share, total_cols, extent_y), (3 * HALF, HALF)], "first")(
            gram_one, matrix)
    gram_two = reduce_all(part_two, "sum_second", 2)
    own_rows, factor = call(
        functools.partial(second_kernel, root_rows, groups),
        [(blocks, local_cols, extent_y), square], "second",
        [square, (blocks - share, total_cols, extent_y)])(
            gram_two, upper_one, lower_one, ortho_once, matrix, *rest)
    basis = own_rows.reshape(extent_x, comps, local_cols, extent_y).transpose(2, 1, 0, 3)
    aa, ab, bb = gram_one[:HALF], gram_one[HALF : 2 * HALF], gram_one[2 * HALF :]
    gram = jnp.concatenate(
        [jnp.concatenate([aa, ab], axis=1), jnp.concatenate([ab.T, bb], axis=1)], axis=0)
    return (basis, factor, gram / row_count)


def solution(mesh):
    in_specs = (
        P("skc", None, "prow", "pcol"),
        P("prow", "pcol"),
        P(None, "prow", "pcol"),
        P(),
        P(),
    )
    out_specs = (P("skc", None, "prow", "pcol"), P(), P())
    return jax.shard_map(body, mesh=mesh, in_specs=in_specs, out_specs=out_specs, check_vma=False)
```

```python
import functools
import math

import jax
import jax.numpy as jnp
from jax import lax
from jax.experimental import pallas as pl
from jax.experimental.pallas import tpu as pltpu
from jax.sharding import PartitionSpec as P

MESH = pl.DeviceIdType.MESH
HIGHEST = lax.Precision.HIGHEST
HALF = 128
CHUNKS = 2


def dot(a, b, dims, precision=HIGHEST):
    return lax.dot_general(
        a, b, (dims, ((), ())), precision=precision, preferred_element_type=jnp.float32
    )


NN = ((1,), (0,))
NT = ((1,), (1,))
TN = ((0,), (0,))


def reduce_kernel(planes, cols, rows, part_ref, out_ref, plane_buf, row_buf,
                  send_a, recv_a, send_b, recv_b, send_c, recv_c):
    me = lax.axis_index("pcol") * cols + lax.axis_index("skc")
    row = lax.axis_index("prow")
    chunk = part_ref.shape[0] // planes

    def at_plane(t):
        return {"pcol": t // cols, "skc": t % cols}

    def piece(ref, t):
        return ref.at[pl.ds(pl.multiple_of(t * chunk, 8), chunk)]

    others = [lax.rem(me + o, planes) for o in range(1, planes)]
    other_rows = [lax.rem(row + o, rows) for o in range(1, rows)]
    barrier = pltpu.get_barrier_semaphore()
    for t in others:
        pl.semaphore_signal(barrier, inc=1, device_id=at_plane(t), device_id_type=MESH)
    for t in other_rows:
        pl.semaphore_signal(barrier, inc=1, device_id={"prow": t}, device_id_type=MESH)
    pl.semaphore_wait(barrier, planes + rows - 2)

    def exchange(targets, where, source, target, mine, send, recv):
        sent = [
            pltpu.make_async_remote_copy(
                src_ref=source(t), dst_ref=target(mine), send_sem=send.at[t],
                recv_sem=recv.at[mine], device_id=where(t), device_id_type=MESH)
            for t in targets
        ]
        for copy in sent:
            copy.start()
        for t in targets:
            pltpu.make_async_remote_copy(
                src_ref=source(t), dst_ref=target(t), send_sem=send.at[t],
                recv_sem=recv.at[t], device_id=where(t), device_id_type=MESH).wait_recv()
        return sent

    sent = exchange(others, at_plane, lambda t: piece(part_ref, t), lambda t: plane_buf.at[t],
                    me, send_a, recv_a)
    plane_buf[me] = piece(part_ref, me)[...]
    total = plane_buf[0]
    for t in range(1, planes):
        total = total + plane_buf[t]
    row_buf[row] = total
    sent += exchange(other_rows, lambda t: {"prow": t}, lambda t: row_buf.at[row],
                     lambda t: row_buf.at[t], row, send_b, recv_b)
    total = row_buf[0]
    for t in range(1, rows):
        total = total + row_buf[t]
    piece(out_ref, me)[...] = total
    sent += exchange(others, at_plane, lambda t: piece(out_ref, me), lambda t: piece(out_ref, t),
                     me, send_c, recv_c)
    for copy in sent:
        copy.wait_send()


def reduce_all(part, name, collective_id):
    cols, rows = lax.axis_size("skc"), lax.axis_size("prow")
    planes = cols * lax.axis_size("pcol")
    chunk = part.shape[0] // planes
    dma = pltpu.SemaphoreType.DMA
    return pl.pallas_call(
        functools.partial(reduce_kernel, planes, cols, rows),
        out_shape=jax.ShapeDtypeStruct(part.shape, jnp.float32),
        in_specs=[pl.BlockSpec(memory_space=pltpu.VMEM)],
        out_specs=pl.BlockSpec(memory_space=pltpu.VMEM),
        scratch_shapes=[
            pltpu.VMEM((planes, chunk, part.shape[1]), jnp.float32),
            pltpu.VMEM((rows, chunk, part.shape[1]), jnp.float32),
            dma((planes,)), dma((planes,)), dma((rows,)), dma((rows,)),
            dma((planes,)), dma((planes,)),
        ],
        compiler_params=pltpu.CompilerParams(collective_id=collective_id, has_side_effects=True),
        name=name,
    )(part)


def eliminate(block):
    size = block.shape[0]
    tiles = size // 8
    lanes = lax.broadcasted_iota(jnp.int32, (8, size), 1)
    subs = lax.broadcasted_iota(jnp.int32, (8, size), 0)
    left = [block[8 * t : 8 * t + 8] for t in range(tiles)]
    right = [jnp.where(lanes == subs + 8 * t, 1.0, 0.0).astype(jnp.float32) for t in range(tiles)]

    def columns(tile, t):
        return [jnp.broadcast_to(tile[:, 8 * t + c : 8 * t + c + 1], (8, size)) for c in range(8)]

    def row(tile, s):
        return jnp.broadcast_to(tile[s : s + 1], (8, size))

    scales = []
    for t in range(tiles):
        cols = columns(left[t], t)
        inverses, pivots, rows_l, rows_r = [], [], [], []
        scale = None
        for s in range(8):
            pivot = row(cols[s], s)
            inverse = 1.0 / pivot
            scale = pivot if scale is None else jnp.where(subs == s, pivot, scale)
            rows_l.append(row(left[t], s))
            rows_r.append(row(right[t], s))
            inverses.append(inverse)
            if s == 7:
                pivots.append([])
                break
            factor = jnp.where(subs > s, cols[s] * inverse, 0.0)
            heads = [row(cols[c], s) for c in range(s + 1, 8)]
            pivots.append(heads)
            for c in range(s + 1, 8):
                cols[c] = cols[c] - factor * heads[c - s - 1]
            left[t] = left[t] - factor * rows_l[s]
            right[t] = right[t] - factor * rows_r[s]
        scales.append(lax.rsqrt(scale))
        for v in range(t + 1, tiles):
            cols = columns(left[v], t)
            for s in range(8):
                factor = cols[s] * inverses[s]
                for c in range(s + 1, 8):
                    cols[c] = cols[c] - factor * pivots[s][c - s - 1]
                left[v] = left[v] - factor * rows_l[s]
                right[v] = right[v] - factor * rows_r[s]
    upper = [jnp.where(lanes >= subs + 8 * t, left[t] * scales[t], 0.0) for t in range(tiles)]
    lower = [right[t] * scales[t] for t in range(tiles)]
    return jnp.concatenate(upper, axis=0), jnp.concatenate(lower, axis=0)


def factorize(gram_ref):
    h = HALF
    r11, i11 = eliminate(gram_ref[0:h])
    r12 = dot(i11, gram_ref[h : 2 * h], NN)
    r22, i22 = eliminate(gram_ref[2 * h : 3 * h] - dot(r12, r12, TN))
    i21 = -dot(i22, dot(r12, i11, TN), NN)
    zero = jnp.zeros((h, h), jnp.float32)
    upper = jnp.concatenate(
        [jnp.concatenate([r11, r12], axis=1), jnp.concatenate([zero, r22], axis=1)], axis=0)
    lower = jnp.concatenate(
        [jnp.concatenate([i11, zero], axis=1), jnp.concatenate([i21, i22], axis=1)], axis=0)
    return upper, lower


def sketch_kernel(cols, rows, planes, field_ref, modulus_ref, coupling_ref,
                  matrix_ref, part_ref, once, above, below, edges, arrived, halo,
                  send_row, recv_row, send_col, recv_col, send_skc, recv_skc):
    extent, comps, count, width = field_ref.shape
    blocks = extent * comps
    mine = lax.axis_index("skc")
    row, col = lax.axis_index("prow"), lax.axis_index("pcol")
    has = {-1: row > 0, 0: None, 1: row < rows - 1}
    has_col = {-1: col > 0, 1: col < planes - 1}
    corners = [(a, b) for b in (-1, 1) for a in (-1, 0, 1)]

    def exists(a, b):
        if b == 0:
            return has[a]
        return has_col[b] if a == 0 else jnp.logical_and(has[a], has_col[b])

    def at(a, b):
        return {"prow": row + a, "pcol": col + b}

    def skc_peer(o):
        return lax.rem(mine + o, cols)

    directions = corners + [(-1, 0), (1, 0)]
    above[...] = jnp.zeros_like(above)
    below[...] = jnp.zeros_like(below)
    arrived[...] = jnp.zeros_like(arrived)
    barrier = pltpu.get_barrier_semaphore()
    for a, b in directions:
        @pl.when(exists(a, b))
        def _():
            pl.semaphore_signal(barrier, inc=1, device_id=at(a, b), device_id_type=MESH)
    for o in range(1, cols):
        pl.semaphore_signal(barrier, inc=1, device_id={"skc": skc_peer(o)}, device_id_type=MESH)
    ends = [jnp.where(row > 0, 1, 0) + jnp.where(row < rows - 1, 1, 0),
            jnp.where(col > 0, 1, 0) + jnp.where(col < planes - 1, 1, 0)]
    pl.semaphore_wait(barrier, (ends[0] + 1) * (ends[1] + 1) - 1 + cols - 1)

    lanes = lax.broadcasted_iota(jnp.int32, (8, width), 1)
    wide = lax.broadcasted_iota(jnp.int32, (count, width), 1)

    length = count // CHUNKS

    def row_copy(source, step, a, c):
        index = CHUNKS * (2 * step + (0 if a < 0 else 1)) + c
        target = below if a < 0 else above
        span = pl.ds(c * length, length)
        return pltpu.make_async_remote_copy(
            src_ref=source.at[0 if a < 0 else extent - 1, :, span],
            dst_ref=target.at[step, :, span],
            send_sem=send_row.at[index], recv_sem=recv_row.at[index],
            device_id=at(a, 0), device_id_type=MESH)

    def col_copy(step, a, b):
        index = 6 * step + corners.index((a, b))
        return pltpu.make_async_remote_copy(
            src_ref=edges.at[2 * step + (0 if b < 0 else 1)], dst_ref=arrived.at[index],
            send_sem=send_col.at[index], recv_sem=recv_col.at[index],
            device_id=at(a, b), device_id_type=MESH)

    def start_rows(source, step, c):
        for a in (-1, 1):
            @pl.when(exists(a, 0))
            def _():
                row_copy(source, step, a, c).start()

    def wait_rows(source, step, c):
        for a in (-1, 1):
            @pl.when(exists(-a, 0))
            def _():
                row_copy(source, step, a, c).wait_recv()

    def exchange_edges(source, step):
        for b in (-1, 1):
            packed = jnp.zeros((count, width), jnp.float32)
            for p in range(blocks):
                place = source[p // comps, p % comps]
                edge = place[:, 0:1] if b < 0 else place[:, width - 1 : width]
                packed = jnp.where(wide == p, edge, packed)
            edges[2 * step + (0 if b < 0 else 1)] = packed.T[: edges.shape[1]]
        for a, b in corners:
            @pl.when(exists(a, b))
            def _():
                col_copy(step, a, b).start()
        for a, b in corners:
            @pl.when(exists(-a, -b))
            def _():
                col_copy(step, a, b).wait_recv()
        pad = jnp.zeros((width - blocks - 2 * comps, count), jnp.float32)
        for b in (-1, 1):
            index = 6 * step
            centre = arrived[index + corners.index((0, b))][:blocks]
            upper = arrived[index + corners.index((1, b))][blocks - comps : blocks]
            under = arrived[index + corners.index((-1, b))][:comps]
            halo[0 if b > 0 else 1] = jnp.concatenate([upper, centre, under, pad], axis=0).T

    def apply(source, step, store, chunk):
        def tile(k, carry):
            at_k = pl.ds(pl.multiple_of(k * 8, 8), 8)
            acc = [[source[x, i, at_k] for x in range(extent)] for i in range(comps)]
            before, after = halo[0, at_k], halo[1, at_k]
            for j in range(comps):
                plain = [above[step, j, at_k]] + [source[x, j, at_k] for x in range(extent)]
                plain.append(below[step, j, at_k])
                for c in range(3):
                    if c == 1:
                        shifted = plain
                    else:
                        edge, hide, turn = (before, 0, 1) if c == 0 else (after, width - 1, width - 1)
                        shifted = [
                            jnp.where(lanes == hide, edge[:, comps * x + j : comps * x + j + 1],
                                      pltpu.roll(plain[x], turn, 1))
                            for x in range(extent + 2)
                        ]
                    for r in range(3):
                        for i in range(comps):
                            weight = coupling_ref[(3 * r + c) * comps * comps + i * comps + j]
                            for x in range(extent):
                                acc[i][x] = acc[i][x] + weight * shifted[x + r]
            for i in range(comps):
                for x in range(extent):
                    store(x, i, k, modulus_ref[x : x + 1, :] * acc[i][x])
            return carry

        lax.fori_loop(chunk * length // 8, (chunk + 1) * length // 8, tile, 0)

    def store_once(x, i, k, value):
        once[x, i, pl.ds(pl.multiple_of(k * 8, 8), 8)] = value

    def store_last(x, i, k, value):
        start = pl.multiple_of(mine * count + k * 8, 8)
        matrix_ref[comps * x + i, pl.ds(start, 8)] = value

    share = blocks // cols

    def skc_copy(owner, to, part, o, c):
        start = pl.multiple_of(owner * count + c * length, 8)
        place = matrix_ref.at[pl.ds(part * share, share), pl.ds(start, length)]
        index = CHUNKS * (o - 1) + c
        return pltpu.make_async_remote_copy(
            src_ref=place, dst_ref=place, send_sem=send_skc.at[index],
            recv_sem=recv_skc.at[index], device_id={"skc": to}, device_id_type=MESH)

    pairs = [(o, c) for c in range(CHUNKS) for o in range(1, cols)]
    for c in range(CHUNKS):
        start_rows(field_ref, 0, c)
    exchange_edges(field_ref, 0)
    for c in range(CHUNKS):
        wait_rows(field_ref, 0, c)
        apply(field_ref, 0, store_once, c)
        start_rows(once, 1, c)
    exchange_edges(once, 1)
    for c in range(CHUNKS):
        wait_rows(once, 1, c)
        apply(once, 1, store_last, c)
        for o in range(1, cols):
            skc_copy(mine, skc_peer(o), skc_peer(o), o, c).start()
    for o, c in pairs:
        owner = lax.rem(mine + cols - o, cols)
        skc_copy(owner, owner, mine, o, c).wait_recv()
    part_ref[...] = pack_blocks(matrix_ref, mine * share, share)
    for o, c in pairs:
        skc_copy(mine, skc_peer(o), skc_peer(o), o, c).wait_send()
    for step in range(2):
        source = field_ref if step == 0 else once
        for a in (-1, 1):
            @pl.when(exists(a, 0))
            def _():
                for c in range(CHUNKS):
                    row_copy(source, step, a, c).wait_send()
        for a, b in corners:
            @pl.when(exists(a, b))
            def _():
                col_copy(step, a, b).wait_send()


def pack_blocks(ref, start, share):
    total = None
    for p in range(share):
        block = ref[start + p]
        first, second = block[:HALF], block[HALF:]
        terms = [dot(first, first, NT), dot(first, second, NT), dot(second, second, NT)]
        total = terms if total is None else [s + t for s, t in zip(total, terms)]
    return jnp.concatenate(total, axis=0)


def sketch(field, modulus, coupling):
    extent, comps, count, width = field.shape
    cols, rows, planes = (lax.axis_size(a) for a in ("skc", "prow", "pcol"))
    blocks = extent * comps
    edge_rows = -(-blocks // 8) * 8
    dma = pltpu.SemaphoreType.DMA
    vmem = pl.BlockSpec(memory_space=pltpu.VMEM)
    f32 = jnp.float32
    return pl.pallas_call(
        functools.partial(sketch_kernel, cols, rows, planes),
        out_shape=[
            jax.ShapeDtypeStruct((blocks, count * cols, width), f32),
            jax.ShapeDtypeStruct((3 * HALF, HALF), f32),
        ],
        in_specs=[vmem, vmem, pl.BlockSpec(memory_space=pltpu.SMEM)],
        out_specs=[vmem, vmem],
        scratch_shapes=[
            pltpu.VMEM((extent, comps, count, width), f32),
            pltpu.VMEM((2, comps, count, width), f32),
            pltpu.VMEM((2, comps, count, width), f32),
            pltpu.VMEM((4, edge_rows, count), f32),
            pltpu.VMEM((12, edge_rows, count), f32),
            pltpu.VMEM((2, count, width), f32),
            dma((4 * CHUNKS,)), dma((4 * CHUNKS,)), dma((12,)), dma((12,)),
            dma((CHUNKS * (cols - 1),)), dma((CHUNKS * (cols - 1),)),
        ],
        compiler_params=pltpu.CompilerParams(
            collective_id=3, has_side_effects=True, vmem_limit_bytes=40 * 1024 * 1024),
        name="sketch",
    )(field, modulus, coupling)


def first_kernel(groups, gram_ref, matrix_ref, upper_ref, lower_ref, ortho_ref, part_ref):
    upper, lower = factorize(gram_ref)
    upper_ref[...] = upper
    lower_ref[...] = lower
    share = matrix_ref.shape[0] // groups
    start = lax.axis_index("skc") * share
    for p in range(share):
        ortho_ref[p] = dot(lower, matrix_ref[start + p], NN)
    part_ref[...] = pack_blocks(ortho_ref, 0, share)


def second_kernel(scale, groups, gram_ref, upper_one_ref, lower_one_ref, ortho_ref, matrix_ref,
                  *refs):
    rest, (out_ref, factor_ref, lower_ref, block_ref) = refs[: groups - 1], refs[groups - 1 :]
    upper, lower = factorize(gram_ref)
    factor_ref[...] = dot(upper, upper_one_ref[...], NN) * (1.0 / scale)
    count = lower.shape[0] // groups
    mine = lax.axis_index("skc")
    share = ortho_ref.shape[0]
    lower_ref[...] = lower * scale
    place = pl.ds(pl.multiple_of(mine * count, 8), count)
    own = lower_ref[place]
    for p in range(share):
        out_ref[mine * share + p] = dot(own, ortho_ref[p], NN)
    both = dot(own, lower_one_ref[...], NN)
    for q in range(1, groups):
        start = lax.rem(mine + q, groups) * share
        for p in range(share):
            slot = (q - 1) * share + p
            block_ref[slot, place] = matrix_ref[start + p, place]
            for o in range(1, groups):
                owner = lax.rem(mine + groups - o, groups)
                there = pl.ds(pl.multiple_of(owner * count, 8), count)
                block_ref[slot, there] = rest[o - 1][slot]
            out_ref[start + p] = dot(both, block_ref[slot], NN)


def call(kernel, outs, name, scratch=()):
    return pl.pallas_call(
        kernel,
        out_shape=[jax.ShapeDtypeStruct(s, jnp.float32) for s in outs],
        scratch_shapes=[pltpu.VMEM(s, jnp.float32) for s in scratch],
        compiler_params=pltpu.CompilerParams(vmem_limit_bytes=40 * 1024 * 1024),
        cost_estimate=pl.CostEstimate(
            flops=5 * 10**9, bytes_accessed=4 * 10**7, transcendentals=0),
        name=name,
    )


def remaining(matrix, count, groups):
    share = matrix.shape[0] // groups
    mine = lax.axis_index("skc")
    for offset in range(1, groups):
        to = lax.rem(mine + offset, groups)
        pieces = [
            lax.dynamic_slice(
                matrix, (lax.rem(to + q, groups) * share, mine * count, 0),
                (share, count, matrix.shape[2]))
            for q in range(1, groups)
        ]
        payload = pieces[0] if groups == 2 else jnp.concatenate(pieces, axis=0)
        yield lax.ppermute(payload, "skc", [(i, (i + offset) % groups) for i in range(groups)])


def body(omega, elastic, prony, prony_weight, coupling):
    modulus = elastic + jnp.sum(prony_weight[:, None, None] * prony, axis=0)
    local_cols, comps, extent_x, extent_y = omega.shape
    groups = lax.axis_size("skc")
    total_cols = local_cols * groups
    blocks = comps * extent_x
    row_count = blocks * extent_y * lax.axis_size("prow") * lax.axis_size("pcol")
    root_rows = math.sqrt(row_count)
    matrix, part_one = sketch(omega.transpose(2, 1, 0, 3), modulus, coupling.reshape(-1))
    gram_one = reduce_all(part_one, "sum_first", 1)
    gram_one, later = lax.optimization_barrier((gram_one, matrix))
    rest = list(remaining(later, local_cols, groups))
    square = (total_cols, total_cols)
    share = blocks // groups
    upper_one, lower_one, ortho_once, part_two = call(
        functools.partial(first_kernel, groups),
        [square, square, (share, total_cols, extent_y), (3 * HALF, HALF)], "first")(
            gram_one, matrix)
    gram_two = reduce_all(part_two, "sum_second", 2)
    own_rows, factor = call(
        functools.partial(second_kernel, root_rows, groups),
        [(blocks, local_cols, extent_y), square], "second",
        [square, (blocks - share, total_cols, extent_y)])(
            gram_two, upper_one, lower_one, ortho_once, matrix, *rest)
    basis = own_rows.reshape(extent_x, comps, local_cols, extent_y).transpose(2, 1, 0, 3)
    aa, ab, bb = gram_one[:HALF], gram_one[HALF : 2 * HALF], gram_one[2 * HALF :]
    gram = jnp.concatenate(
        [jnp.concatenate([aa, ab], axis=1), jnp.concatenate([ab.T, bb], axis=1)], axis=0)
    return (basis, factor, gram / row_count)


def solution(mesh):
    in_specs = (
        P("skc", None, "prow", "pcol"),
        P("prow", "pcol"),
        P(None, "prow", "pcol"),
        P(),
        P(),
    )
    out_specs = (P("skc", None, "prow", "pcol"), P(), P())
    return jax.shard_map(body, mesh=mesh, in_specs=in_specs, out_specs=out_specs, check_vma=False)
```

```python
import functools
import math

import jax
import jax.numpy as jnp
from jax import lax
from jax.experimental import pallas as pl
from jax.experimental.pallas import tpu as pltpu
from jax.sharding import PartitionSpec as P

MESH = pl.DeviceIdType.MESH
HIGHEST = lax.Precision.HIGHEST
HALF = 128
CHUNKS = 4


def dot(a, b, dims, precision=HIGHEST):
    return lax.dot_general(
        a, b, (dims, ((), ())), precision=precision, preferred_element_type=jnp.float32
    )


NN = ((1,), (0,))
NT = ((1,), (1,))
TN = ((0,), (0,))


def reduce_kernel(planes, cols, rows, part_ref, out_ref, plane_buf, row_buf,
                  send_a, recv_a, send_b, recv_b, send_c, recv_c):
    me = lax.axis_index("pcol") * cols + lax.axis_index("skc")
    row = lax.axis_index("prow")
    chunk = part_ref.shape[0] // planes

    def at_plane(t):
        return {"pcol": t // cols, "skc": t % cols}

    def piece(ref, t):
        return ref.at[pl.ds(pl.multiple_of(t * chunk, 8), chunk)]

    others = [lax.rem(me + o, planes) for o in range(1, planes)]
    other_rows = [lax.rem(row + o, rows) for o in range(1, rows)]
    barrier = pltpu.get_barrier_semaphore()
    for t in others:
        pl.semaphore_signal(barrier, inc=1, device_id=at_plane(t), device_id_type=MESH)
    for t in other_rows:
        pl.semaphore_signal(barrier, inc=1, device_id={"prow": t}, device_id_type=MESH)
    pl.semaphore_wait(barrier, planes + rows - 2)

    def exchange(targets, where, source, target, mine, send, recv):
        sent = [
            pltpu.make_async_remote_copy(
                src_ref=source(t), dst_ref=target(mine), send_sem=send.at[t],
                recv_sem=recv.at[mine], device_id=where(t), device_id_type=MESH)
            for t in targets
        ]
        for copy in sent:
            copy.start()
        for t in targets:
            pltpu.make_async_remote_copy(
                src_ref=source(t), dst_ref=target(t), send_sem=send.at[t],
                recv_sem=recv.at[t], device_id=where(t), device_id_type=MESH).wait_recv()
        return sent

    sent = exchange(others, at_plane, lambda t: piece(part_ref, t), lambda t: plane_buf.at[t],
                    me, send_a, recv_a)
    plane_buf[me] = piece(part_ref, me)[...]
    total = plane_buf[0]
    for t in range(1, planes):
        total = total + plane_buf[t]
    row_buf[row] = total
    sent += exchange(other_rows, lambda t: {"prow": t}, lambda t: row_buf.at[row],
                     lambda t: row_buf.at[t], row, send_b, recv_b)
    total = row_buf[0]
    for t in range(1, rows):
        total = total + row_buf[t]
    piece(out_ref, me)[...] = total
    sent += exchange(others, at_plane, lambda t: piece(out_ref, me), lambda t: piece(out_ref, t),
                     me, send_c, recv_c)
    for copy in sent:
        copy.wait_send()


def reduce_all(part, name, collective_id):
    cols, rows = lax.axis_size("skc"), lax.axis_size("prow")
    planes = cols * lax.axis_size("pcol")
    chunk = part.shape[0] // planes
    dma = pltpu.SemaphoreType.DMA
    return pl.pallas_call(
        functools.partial(reduce_kernel, planes, cols, rows),
        out_shape=jax.ShapeDtypeStruct(part.shape, jnp.float32),
        in_specs=[pl.BlockSpec(memory_space=pltpu.VMEM)],
        out_specs=pl.BlockSpec(memory_space=pltpu.VMEM),
        scratch_shapes=[
            pltpu.VMEM((planes, chunk, part.shape[1]), jnp.float32),
            pltpu.VMEM((rows, chunk, part.shape[1]), jnp.float32),
            dma((planes,)), dma((planes,)), dma((rows,)), dma((rows,)),
            dma((planes,)), dma((planes,)),
        ],
        compiler_params=pltpu.CompilerParams(collective_id=collective_id, has_side_effects=True),
        name=name,
    )(part)


def eliminate(block):
    size = block.shape[0]
    tiles = size // 8
    lanes = lax.broadcasted_iota(jnp.int32, (8, size), 1)
    subs = lax.broadcasted_iota(jnp.int32, (8, size), 0)
    left = [block[8 * t : 8 * t + 8] for t in range(tiles)]
    right = [jnp.where(lanes == subs + 8 * t, 1.0, 0.0).astype(jnp.float32) for t in range(tiles)]

    def columns(tile, t):
        return [jnp.broadcast_to(tile[:, 8 * t + c : 8 * t + c + 1], (8, size)) for c in range(8)]

    def row(tile, s):
        return jnp.broadcast_to(tile[s : s + 1], (8, size))

    scales = []
    for t in range(tiles):
        cols = columns(left[t], t)
        inverses, pivots, rows_l, rows_r = [], [], [], []
        scale = None
        for s in range(8):
            pivot = row(cols[s], s)
            inverse = 1.0 / pivot
            scale = pivot if scale is None else jnp.where(subs == s, pivot, scale)
            rows_l.append(row(left[t], s))
            rows_r.append(row(right[t], s))
            inverses.append(inverse)
            if s == 7:
                pivots.append([])
                break
            factor = jnp.where(subs > s, cols[s] * inverse, 0.0)
            heads = [row(cols[c], s) for c in range(s + 1, 8)]
            pivots.append(heads)
            for c in range(s + 1, 8):
                cols[c] = cols[c] - factor * heads[c - s - 1]
            left[t] = left[t] - factor * rows_l[s]
            right[t] = right[t] - factor * rows_r[s]
        scales.append(lax.rsqrt(scale))
        for v in range(t + 1, tiles):
            cols = columns(left[v], t)
            for s in range(8):
                factor = cols[s] * inverses[s]
                for c in range(s + 1, 8):
                    cols[c] = cols[c] - factor * pivots[s][c - s - 1]
                left[v] = left[v] - factor * rows_l[s]
                right[v] = right[v] - factor * rows_r[s]
    upper = [jnp.where(lanes >= subs + 8 * t, left[t] * scales[t], 0.0) for t in range(tiles)]
    lower = [right[t] * scales[t] for t in range(tiles)]
    return jnp.concatenate(upper, axis=0), jnp.concatenate(lower, axis=0)


def factorize(gram_ref):
    h = HALF
    r11, i11 = eliminate(gram_ref[0:h])
    r12 = dot(i11, gram_ref[h : 2 * h], NN)
    r22, i22 = eliminate(gram_ref[2 * h : 3 * h] - dot(r12, r12, TN))
    i21 = -dot(i22, dot(r12, i11, TN), NN)
    zero = jnp.zeros((h, h), jnp.float32)
    upper = jnp.concatenate(
        [jnp.concatenate([r11, r12], axis=1), jnp.concatenate([zero, r22], axis=1)], axis=0)
    lower = jnp.concatenate(
        [jnp.concatenate([i11, zero], axis=1), jnp.concatenate([i21, i22], axis=1)], axis=0)
    return upper, lower


def sketch_kernel(cols, rows, planes, field_ref, modulus_ref, coupling_ref,
                  matrix_ref, part_ref, once, above, below, edges, arrived, halo,
                  send_row, recv_row, send_col, recv_col, send_skc, recv_skc):
    extent, comps, count, width = field_ref.shape
    blocks = extent * comps
    mine = lax.axis_index("skc")
    row, col = lax.axis_index("prow"), lax.axis_index("pcol")
    has = {-1: row > 0, 0: None, 1: row < rows - 1}
    has_col = {-1: col > 0, 1: col < planes - 1}
    corners = [(a, b) for b in (-1, 1) for a in (-1, 0, 1)]

    def exists(a, b):
        if b == 0:
            return has[a]
        return has_col[b] if a == 0 else jnp.logical_and(has[a], has_col[b])

    def at(a, b):
        return {"prow": row + a, "pcol": col + b}

    def skc_peer(o):
        return lax.rem(mine + o, cols)

    directions = corners + [(-1, 0), (1, 0)]
    above[...] = jnp.zeros_like(above)
    below[...] = jnp.zeros_like(below)
    arrived[...] = jnp.zeros_like(arrived)
    barrier = pltpu.get_barrier_semaphore()
    for a, b in directions:
        @pl.when(exists(a, b))
        def _():
            pl.semaphore_signal(barrier, inc=1, device_id=at(a, b), device_id_type=MESH)
    for o in range(1, cols):
        pl.semaphore_signal(barrier, inc=1, device_id={"skc": skc_peer(o)}, device_id_type=MESH)
    ends = [jnp.where(row > 0, 1, 0) + jnp.where(row < rows - 1, 1, 0),
            jnp.where(col > 0, 1, 0) + jnp.where(col < planes - 1, 1, 0)]
    pl.semaphore_wait(barrier, (ends[0] + 1) * (ends[1] + 1) - 1 + cols - 1)

    lanes = lax.broadcasted_iota(jnp.int32, (8, width), 1)
    wide = lax.broadcasted_iota(jnp.int32, (count, width), 1)

    length = count // CHUNKS

    def row_copy(source, step, a, c):
        index = CHUNKS * (2 * step + (0 if a < 0 else 1)) + c
        target = below if a < 0 else above
        span = pl.ds(c * length, length)
        return pltpu.make_async_remote_copy(
            src_ref=source.at[0 if a < 0 else extent - 1, :, span],
            dst_ref=target.at[step, :, span],
            send_sem=send_row.at[index], recv_sem=recv_row.at[index],
            device_id=at(a, 0), device_id_type=MESH)

    def col_copy(step, a, b):
        index = 6 * step + corners.index((a, b))
        return pltpu.make_async_remote_copy(
            src_ref=edges.at[2 * step + (0 if b < 0 else 1)], dst_ref=arrived.at[index],
            send_sem=send_col.at[index], recv_sem=recv_col.at[index],
            device_id=at(a, b), device_id_type=MESH)

    def start_rows(source, step, c):
        for a in (-1, 1):
            @pl.when(exists(a, 0))
            def _():
                row_copy(source, step, a, c).start()

    def wait_rows(source, step, c):
        for a in (-1, 1):
            @pl.when(exists(-a, 0))
            def _():
                row_copy(source, step, a, c).wait_recv()

    def exchange_edges(source, step):
        for b in (-1, 1):
            packed = jnp.zeros((count, width), jnp.float32)
            for p in range(blocks):
                place = source[p // comps, p % comps]
                edge = place[:, 0:1] if b < 0 else place[:, width - 1 : width]
                packed = jnp.where(wide == p, edge, packed)
            edges[2 * step + (0 if b < 0 else 1)] = packed.T[: edges.shape[1]]
        for a, b in corners:
            @pl.when(exists(a, b))
            def _():
                col_copy(step, a, b).start()
        for a, b in corners:
            @pl.when(exists(-a, -b))
            def _():
                col_copy(step, a, b).wait_recv()
        pad = jnp.zeros((width - blocks - 2 * comps, count), jnp.float32)
        for b in (-1, 1):
            index = 6 * step
            centre = arrived[index + corners.index((0, b))][:blocks]
            upper = arrived[index + corners.index((1, b))][blocks - comps : blocks]
            under = arrived[index + corners.index((-1, b))][:comps]
            halo[0 if b > 0 else 1] = jnp.concatenate([upper, centre, under, pad], axis=0).T

    def apply(source, step, store, chunk):
        def tile(k, carry):
            at_k = pl.ds(pl.multiple_of(k * 8, 8), 8)
            acc = [[source[x, i, at_k] for x in range(extent)] for i in range(comps)]
            before, after = halo[0, at_k], halo[1, at_k]
            for j in range(comps):
                plain = [above[step, j, at_k]] + [source[x, j, at_k] for x in range(extent)]
                plain.append(below[step, j, at_k])
                for c in range(3):
                    if c == 1:
                        shifted = plain
                    else:
                        edge, hide, turn = (before, 0, 1) if c == 0 else (after, width - 1, width - 1)
                        shifted = [
                            jnp.where(lanes == hide, edge[:, comps * x + j : comps * x + j + 1],
                                      pltpu.roll(plain[x], turn, 1))
                            for x in range(extent + 2)
                        ]
                    for r in range(3):
                        for i in range(comps):
                            weight = coupling_ref[(3 * r + c) * comps * comps + i * comps + j]
                            for x in range(extent):
                                acc[i][x] = acc[i][x] + weight * shifted[x + r]
            for i in range(comps):
                for x in range(extent):
                    store(x, i, k, modulus_ref[x : x + 1, :] * acc[i][x])
            return carry

        lax.fori_loop(chunk * length // 8, (chunk + 1) * length // 8, tile, 0)

    def store_once(x, i, k, value):
        once[x, i, pl.ds(pl.multiple_of(k * 8, 8), 8)] = value

    def store_last(x, i, k, value):
        start = pl.multiple_of(mine * count + k * 8, 8)
        matrix_ref[comps * x + i, pl.ds(start, 8)] = value

    share = blocks // cols

    def skc_copy(owner, to, part, o, c):
        start = pl.multiple_of(owner * count + c * length, 8)
        place = matrix_ref.at[pl.ds(part * share, share), pl.ds(start, length)]
        index = CHUNKS * (o - 1) + c
        return pltpu.make_async_remote_copy(
            src_ref=place, dst_ref=place, send_sem=send_skc.at[index],
            recv_sem=recv_skc.at[index], device_id={"skc": to}, device_id_type=MESH)

    pairs = [(o, c) for c in range(CHUNKS) for o in range(1, cols)]
    for c in range(CHUNKS):
        start_rows(field_ref, 0, c)
    exchange_edges(field_ref, 0)
    for c in range(CHUNKS):
        wait_rows(field_ref, 0, c)
        apply(field_ref, 0, store_once, c)
        start_rows(once, 1, c)
    exchange_edges(once, 1)
    for c in range(CHUNKS):
        wait_rows(once, 1, c)
        apply(once, 1, store_last, c)
        for o in range(1, cols):
            skc_copy(mine, skc_peer(o), skc_peer(o), o, c).start()
    for o, c in pairs:
        owner = lax.rem(mine + cols - o, cols)
        skc_copy(owner, owner, mine, o, c).wait_recv()
    part_ref[...] = pack_blocks(matrix_ref, mine * share, share)
    for o, c in pairs:
        skc_copy(mine, skc_peer(o), skc_peer(o), o, c).wait_send()
    for step in range(2):
        source = field_ref if step == 0 else once
        for a in (-1, 1):
            @pl.when(exists(a, 0))
            def _():
                for c in range(CHUNKS):
                    row_copy(source, step, a, c).wait_send()
        for a, b in corners:
            @pl.when(exists(a, b))
            def _():
                col_copy(step, a, b).wait_send()


def pack_blocks(ref, start, share):
    total = None
    for p in range(share):
        block = ref[start + p]
        first, second = block[:HALF], block[HALF:]
        terms = [dot(first, first, NT), dot(first, second, NT), dot(second, second, NT)]
        total = terms if total is None else [s + t for s, t in zip(total, terms)]
    return jnp.concatenate(total, axis=0)


def sketch(field, modulus, coupling):
    extent, comps, count, width = field.shape
    cols, rows, planes = (lax.axis_size(a) for a in ("skc", "prow", "pcol"))
    blocks = extent * comps
    edge_rows = -(-blocks // 8) * 8
    dma = pltpu.SemaphoreType.DMA
    vmem = pl.BlockSpec(memory_space=pltpu.VMEM)
    f32 = jnp.float32
    return pl.pallas_call(
        functools.partial(sketch_kernel, cols, rows, planes),
        out_shape=[
            jax.ShapeDtypeStruct((blocks, count * cols, width), f32),
            jax.ShapeDtypeStruct((3 * HALF, HALF), f32),
        ],
        in_specs=[vmem, vmem, pl.BlockSpec(memory_space=pltpu.SMEM)],
        out_specs=[vmem, vmem],
        scratch_shapes=[
            pltpu.VMEM((extent, comps, count, width), f32),
            pltpu.VMEM((2, comps, count, width), f32),
            pltpu.VMEM((2, comps, count, width), f32),
            pltpu.VMEM((4, edge_rows, count), f32),
            pltpu.VMEM((12, edge_rows, count), f32),
            pltpu.VMEM((2, count, width), f32),
            dma((4 * CHUNKS,)), dma((4 * CHUNKS,)), dma((12,)), dma((12,)),
            dma((CHUNKS * (cols - 1),)), dma((CHUNKS * (cols - 1),)),
        ],
        compiler_params=pltpu.CompilerParams(
            collective_id=3, has_side_effects=True, vmem_limit_bytes=40 * 1024 * 1024),
        name="sketch",
    )(field, modulus, coupling)


def first_kernel(groups, gram_ref, matrix_ref, upper_ref, lower_ref, ortho_ref, part_ref):
    upper, lower = factorize(gram_ref)
    upper_ref[...] = upper
    lower_ref[...] = lower
    share = matrix_ref.shape[0] // groups
    start = lax.axis_index("skc") * share
    for p in range(share):
        ortho_ref[p] = dot(lower, matrix_ref[start + p], NN)
    part_ref[...] = pack_blocks(ortho_ref, 0, share)


def second_kernel(scale, groups, gram_ref, upper_one_ref, lower_one_ref, ortho_ref, matrix_ref,
                  *refs):
    rest, (out_ref, factor_ref, lower_ref, block_ref) = refs[: groups - 1], refs[groups - 1 :]
    upper, lower = factorize(gram_ref)
    factor_ref[...] = dot(upper, upper_one_ref[...], NN) * (1.0 / scale)
    count = lower.shape[0] // groups
    mine = lax.axis_index("skc")
    share = ortho_ref.shape[0]
    lower_ref[...] = lower * scale
    place = pl.ds(pl.multiple_of(mine * count, 8), count)
    own = lower_ref[place]
    for p in range(share):
        out_ref[mine * share + p] = dot(own, ortho_ref[p], NN)
    both = dot(own, lower_one_ref[...], NN)
    for q in range(1, groups):
        start = lax.rem(mine + q, groups) * share
        for p in range(share):
            slot = (q - 1) * share + p
            block_ref[slot, place] = matrix_ref[start + p, place]
            for o in range(1, groups):
                owner = lax.rem(mine + groups - o, groups)
                there = pl.ds(pl.multiple_of(owner * count, 8), count)
                block_ref[slot, there] = rest[o - 1][slot]
            out_ref[start + p] = dot(both, block_ref[slot], NN)


def call(kernel, outs, name, scratch=()):
    return pl.pallas_call(
        kernel,
        out_shape=[jax.ShapeDtypeStruct(s, jnp.float32) for s in outs],
        scratch_shapes=[pltpu.VMEM(s, jnp.float32) for s in scratch],
        compiler_params=pltpu.CompilerParams(vmem_limit_bytes=40 * 1024 * 1024),
        cost_estimate=pl.CostEstimate(
            flops=5 * 10**9, bytes_accessed=4 * 10**7, transcendentals=0),
        name=name,
    )


def remaining(matrix, count, groups):
    share = matrix.shape[0] // groups
    mine = lax.axis_index("skc")
    for offset in range(1, groups):
        to = lax.rem(mine + offset, groups)
        pieces = [
            lax.dynamic_slice(
                matrix, (lax.rem(to + q, groups) * share, mine * count, 0),
                (share, count, matrix.shape[2]))
            for q in range(1, groups)
        ]
        payload = pieces[0] if groups == 2 else jnp.concatenate(pieces, axis=0)
        yield lax.ppermute(payload, "skc", [(i, (i + offset) % groups) for i in range(groups)])


def body(omega, elastic, prony, prony_weight, coupling):
    modulus = elastic + jnp.sum(prony_weight[:, None, None] * prony, axis=0)
    local_cols, comps, extent_x, extent_y = omega.shape
    groups = lax.axis_size("skc")
    total_cols = local_cols * groups
    blocks = comps * extent_x
    row_count = blocks * extent_y * lax.axis_size("prow") * lax.axis_size("pcol")
    root_rows = math.sqrt(row_count)
    matrix, part_one = sketch(omega.transpose(2, 1, 0, 3), modulus, coupling.reshape(-1))
    gram_one = reduce_all(part_one, "sum_first", 1)
    gram_one, later = lax.optimization_barrier((gram_one, matrix))
    rest = list(remaining(later, local_cols, groups))
    square = (total_cols, total_cols)
    share = blocks // groups
    upper_one, lower_one, ortho_once, part_two = call(
        functools.partial(first_kernel, groups),
        [square, square, (share, total_cols, extent_y), (3 * HALF, HALF)], "first")(
            gram_one, matrix)
    gram_two = reduce_all(part_two, "sum_second", 2)
    own_rows, factor = call(
        functools.partial(second_kernel, root_rows, groups),
        [(blocks, local_cols, extent_y), square], "second",
        [square, (blocks - share, total_cols, extent_y)])(
            gram_two, upper_one, lower_one, ortho_once, matrix, *rest)
    basis = own_rows.reshape(extent_x, comps, local_cols, extent_y).transpose(2, 1, 0, 3)
    aa, ab, bb = gram_one[:HALF], gram_one[HALF : 2 * HALF], gram_one[2 * HALF :]
    gram = jnp.concatenate(
        [jnp.concatenate([aa, ab], axis=1), jnp.concatenate([ab.T, bb], axis=1)], axis=0)
    return (basis, factor, gram / row_count)


def solution(mesh):
    in_specs = (
        P("skc", None, "prow", "pcol"),
        P("prow", "pcol"),
        P(None, "prow", "pcol"),
        P(),
        P(),
    )
    out_specs = (P("skc", None, "prow", "pcol"), P(), P())
    return jax.shard_map(body, mesh=mesh, in_specs=in_specs, out_specs=out_specs, check_vma=False)
```
